32 devices in a mesh: groups: 2 (over y), slab: 4 (over z), chan: 4 (over x, core).
Axes of the slice: x: 2, y: 2, z: 4, core: 2. Of those that a mesh axis runs over, the one named last changes fastest.
Arguments:
- field: bfloat16 [40, 64, 4, 128, 128], P(('groups', 'chan'), 'slab'), parts along dimension 0, may hold values from -6 to 6
- spec_weight: bfloat16 [20, 20, 1024, 128], P('chan', None, 'slab'), may hold values from -6 to 6
- mix_weight: bfloat16 [20, 20], replicated, may hold values from -1.25 to 1.25
- bias: float32 [20], P('chan'), may hold values from -4 to 4
- cotangent: bfloat16 [40, 64, 4, 128, 128], P(('groups', 'chan'), 'slab'), parts along dimension 0, may hold values from -6 to 6
Outputs:
- output: bfloat16 [40, 64, 4, 128, 128], P(('groups', 'chan'), 'slab'), parts along dimension 0
- grad_field: bfloat16 [40, 64, 4, 128, 128], P(('groups', 'chan'), 'slab'), parts along dimension 0
- grad_weight: bfloat16 [40, 20, 1024, 128], P(('groups', 'chan'), None, 'slab'), parts along dimension 0
The draws below stay inside these ranges and needn't reach their ends.
There are 2 independent parts, one for each index of `groups`. The reference program is written for one: setup_inputs(seed, part) draws one part's arguments, and reference() takes and returns one part's arrays. A program takes and returns all parts, laid end to end along the dimension named above; an argument that names none is the same for every part. Nothing has to cross between parts.
All inputs are finite; a program needn't handle non-finite values.
Results may differ from the reference program's by a relative error of at most 0.023.
Values may be sent and summed in bfloat16 or wider, within the bound.
A program may use at most 256 MiB of HBM per device.

```python
import math
import jax
import jax.numpy as jnp

CH = 20
NX = 128
NY = 128
NZ = 64
NT = 4
KX = 32
KY = 32
KZ = 32
KXY = 1024
KZT = 128


def level_of(own_key, shape, shards, least, largest):
    gain, own = 1.0, jax.random.fold_in(own_key, 6)
    for position, parts in shards:
        heights = jnp.exp(jax.random.uniform(jax.random.fold_in(own, position), (parts,), jnp.float32, least / len(shards), largest / len(shards)))
        gain = gain * jnp.repeat(heights, shape[position] // parts).reshape([-1 if axis == position else 1 for axis in range(len(shape))])
    return gain


def noise(stream_key, shape, scale, reach, shards=(), held_as=jnp.bfloat16):
    drawn = jax.random.normal(stream_key, shape, jnp.float32) * scale
    if len(shards) > 0:
        drawn = level_of(stream_key, shape, shards, -0.22, 0.18) * drawn
    return jnp.clip(drawn, min=-reach, max=reach).astype(held_as)


def setup_inputs(seed: int = 0, part: int = 0) -> dict:
    key_of = jax.random.split(jax.random.key(seed), 6)
    own_keys = jax.random.split(jax.random.fold_in(key_of[5], part), 6)
    return {
        "field": noise(own_keys[0], (CH, NZ, NT, NX, NY), 1.0, 6.0, ((0, 4), (1, 4))),
        "spec_weight": noise(key_of[1], (CH, CH, KXY, KZT), 1.0, 6.0, ((0, 4), (2, 4))),
        "mix_weight": noise(key_of[2], (CH, CH), CH ** -0.5, 1.25),
        "bias": noise(key_of[3], (CH,), 1.0, 4.0, ((0, 4),), jnp.float32),
        "cotangent": noise(own_keys[4], (CH, NZ, NT, NX, NY), 1.0, 6.0, ((0, 4), (1, 4))),
    }


def fourier_rows(count, length):
    rows = jnp.arange(count)
    points = jnp.arange(length)
    freq = (rows + 1) // 2
    phase = freq[:, None] * points[None, :] % length
    angle = phase.astype(jnp.float32) * (2.0 * math.pi / length)
    use_cos = (rows % 2 == 1) | (rows == 0)
    table = jnp.where(use_cos[:, None], jnp.cos(angle), jnp.sin(angle))
    return table * math.sqrt(2.0 / length)

def make_tables():
    table_x = fourier_rows(KX, NX).astype(jnp.bfloat16)
    table_y = fourier_rows(KY, NY).astype(jnp.bfloat16)
    depth = fourier_rows(KZ, NZ)
    times = fourier_rows(NT, NT)
    table_zt = (depth[:, None, :, None] * times[None, :, None, :]).reshape(KZ * NT, NZ * NT)
    return (table_x, table_y, table_zt.astype(jnp.bfloat16))

def as_float(value):
    return value.astype(jnp.float32)

def analyse(values, table_x, table_y, table_zt):
    first = jnp.einsum('cztxy,ky->cztxk', as_float(values), as_float(table_y)).astype(jnp.bfloat16)
    second = jnp.einsum('cztxk,jx->cztjk', as_float(first), as_float(table_x)).astype(jnp.bfloat16)
    second = second.reshape(second.shape[0], NZ * NT, KX * KY)
    return jnp.einsum('mz,czk->ckm', as_float(table_zt), as_float(second)).astype(jnp.bfloat16)

def synthesise(coeffs, table_x, table_y, table_zt):
    slabs = jnp.einsum('mz,okm->ozk', as_float(table_zt), as_float(coeffs)).astype(jnp.bfloat16)
    slabs = slabs.reshape(coeffs.shape[0], NZ, NT, KX, KY)
    first = jnp.einsum('oztjk,jx->oztxk', as_float(slabs), as_float(table_x)).astype(jnp.bfloat16)
    return jnp.einsum('oztxk,ky->oztxy', as_float(first), as_float(table_y))

def reference(field, spec_weight, mix_weight, bias, cotangent):
    table_x, table_y, table_zt = make_tables()
    coeffs = analyse(field, table_x, table_y, table_zt)
    mixed = jnp.einsum('cokm,ckm->okm', as_float(spec_weight), as_float(coeffs)).astype(jnp.bfloat16)
    spectral = synthesise(mixed, table_x, table_y, table_zt)
    pointwise = jnp.einsum('oc,cztxy->oztxy', as_float(mix_weight), as_float(field))
    pre = spectral + pointwise + bias.astype(jnp.float32)[:, None, None, None, None]
    activated, pullback = jax.vjp(jax.nn.gelu, pre)
    output = activated.astype(jnp.bfloat16)
    grad_pre = pullback(as_float(cotangent))[0].astype(jnp.bfloat16)
    grad_coeffs = analyse(grad_pre, table_x, table_y, table_zt)
    grad_weight = (as_float(coeffs)[:, None] * as_float(grad_coeffs)[None]).astype(jnp.bfloat16)
    back_coeffs = jnp.einsum('cokm,okm->ckm', as_float(spec_weight), as_float(grad_coeffs)).astype(jnp.bfloat16)
    back = synthesise(back_coeffs, table_x, table_y, table_zt)
    transposed = jnp.einsum('oc,oztxy->cztxy', as_float(mix_weight), as_float(grad_pre))
    grad_field = (back + transposed).astype(jnp.bfloat16)
    return (output, grad_field, grad_weight)
```

```python
import math

import jax
import jax.numpy as jnp
from jax import lax
from jax.experimental import pallas as pl
from jax.experimental.pallas import tpu as pltpu
from jax.sharding import PartitionSpec as P

NX = 128
NY = 128
NZ = 64
NT = 4
KX = 32
KY = 32
KZ = 32
CHUNKS = 4
TILE = 16
VMEM_BYTES = 40 * 1024 * 1024


def fourier_rows(count, length):
    rows = jnp.arange(count)
    points = jnp.arange(length)
    freq = (rows + 1) // 2
    phase = freq[:, None] * points[None, :] % length
    angle = phase.astype(jnp.float32) * (2.0 * math.pi / length)
    use_cos = (rows % 2 == 1) | (rows == 0)
    table = jnp.where(use_cos[:, None], jnp.cos(angle), jnp.sin(angle))
    return table * math.sqrt(2.0 / length)


def make_tables():
    table_x = fourier_rows(KX, NX).astype(jnp.bfloat16)
    table_y = fourier_rows(KY, NY).astype(jnp.bfloat16)
    depth = fourier_rows(KZ, NZ)
    times = fourier_rows(NT, NT)
    table_zt = (depth[:, None, :, None] * times[None, :, None, :]).reshape(KZ * NT, NZ * NT)
    return (table_x, table_y, table_zt.astype(jnp.bfloat16))


def analyse_xy(values, table_x, table_y):
    first = jnp.einsum(
        "cnxy,ky->cnxk", values, table_y, preferred_element_type=jnp.float32
    ).astype(jnp.bfloat16)
    second = jnp.einsum(
        "cnxk,jx->cnjk", first, table_x, preferred_element_type=jnp.float32
    ).astype(jnp.bfloat16)
    return second.reshape(second.shape[0], second.shape[1], KX * KY)


def analyse_zt(second, table_zt):
    owned = lax.all_to_all(second, "slab", split_axis=2, concat_axis=1, tiled=True)
    return jnp.einsum("mz,czk->ckm", table_zt, owned, preferred_element_type=jnp.float32).astype(
        jnp.bfloat16
    )


def synthesise_zt(coeffs, table_zt):
    slabs = jnp.einsum("mz,okm->ozk", table_zt, coeffs, preferred_element_type=jnp.float32).astype(
        jnp.bfloat16
    )
    local = lax.all_to_all(slabs, "slab", split_axis=1, concat_axis=2, tiled=True)
    count, cells = local.shape[:2]
    local = local.reshape(count, cells, KX, KY).transpose(1, 2, 0, 3)
    return local.reshape(cells, KX, count * KY)


def mix_pair(own_ref, other_ref, weights, row, pair):
    halves = []
    for half in range(2):
        lines = pl.ds((2 * pair + half) * TILE, TILE)
        mine = own_ref[:, row, lines, :]
        theirs = other_ref[:, row, lines, :]
        shape = (mine.shape[0] * TILE, mine.shape[2])
        halves.append(jnp.concatenate([mine.reshape(shape), theirs.reshape(shape)], axis=0))
    return jnp.dot(
        weights, jnp.concatenate(halves, axis=1), preferred_element_type=jnp.float32
    )


def spectral_rows(spec_ref, tx_ref, ty_ref, row):
    first = jnp.dot(tx_ref[...], spec_ref[row], preferred_element_type=jnp.float32)
    return jnp.dot(
        first.astype(jnp.bfloat16), ty_ref[...], preferred_element_type=jnp.float32
    )


def partial_kernel(weight_ref, own_ref, other_ref, out_ref):
    weights = weight_ref[...]
    count, rows, nx, ny = out_ref.shape
    for row in range(rows):
        for pair in range(nx // (2 * TILE)):
            mixed = mix_pair(own_ref, other_ref, weights, row, pair).astype(jnp.bfloat16)
            for half in range(2):
                part = mixed[:, half * ny : (half + 1) * ny]
                out_ref[:, row, pl.ds((2 * pair + half) * TILE, TILE), :] = part.reshape(
                    count, TILE, ny
                )


def forward_kernel(*refs):
    weight_ref, tx_ref, ty_ref, bias_ref, own_ref, other_ref, part_ref, spec_ref, cot_ref = refs[:9]
    out_ref, grad_ref, pre_ref = refs[-3:]
    weights = weight_ref[...]
    count, rows, nx, ny = out_ref.shape
    scale = math.sqrt(2.0 / math.pi)
    cubic = 0.044715
    for row in range(rows):
        pre_ref[...] = spectral_rows(spec_ref, tx_ref, ty_ref, row)
        for pair in range(nx // (2 * TILE)):
            mixed = mix_pair(own_ref, other_ref, weights, row, pair)
            for half in range(2):
                lines = pl.ds((2 * pair + half) * TILE, TILE)
                for o in range(count):
                    pre = (
                        mixed[o * TILE : (o + 1) * TILE, half * ny : (half + 1) * ny]
                        + pre_ref[lines, o * ny : (o + 1) * ny]
                        + part_ref[o, row, lines, :].astype(jnp.float32)
                        + bias_ref[o]
                    )
                    square = pre * pre
                    bent = jnp.tanh(scale * (pre + cubic * (pre * square)))
                    half_up = 0.5 * (1.0 + bent)
                    slope = half_up + (0.5 * pre) * (1.0 - bent * bent) * (
                        scale * (1.0 + (3.0 * cubic) * square)
                    )
                    out_ref[o, row, lines, :] = (pre * half_up).astype(jnp.bfloat16)
                    cot = cot_ref[o, row, lines, :].astype(jnp.float32)
                    grad_ref[o, row, lines, :] = (cot * slope).astype(jnp.bfloat16)


def backward_kernel(*refs):
    weight_ref, tx_ref, ty_ref, own_ref, other_ref, part_ref, spec_ref = refs[:7]
    out_ref, pre_ref = refs[-2:]
    weights = weight_ref[...]
    count, rows, nx, ny = out_ref.shape
    for row in range(rows):
        pre_ref[...] = spectral_rows(spec_ref, tx_ref, ty_ref, row)
        for pair in range(nx // (2 * TILE)):
            mixed = mix_pair(own_ref, other_ref, weights, row, pair)
            for half in range(2):
                lines = pl.ds((2 * pair + half) * TILE, TILE)
                for o in range(count):
                    total = (
                        mixed[o * TILE : (o + 1) * TILE, half * ny : (half + 1) * ny]
                        + pre_ref[lines, o * ny : (o + 1) * ny]
                        + part_ref[o, row, lines, :].astype(jnp.float32)
                    )
                    out_ref[o, row, lines, :] = total.astype(jnp.bfloat16)


class Local:
    def __init__(self, shape):
        self.shape = shape
        self.count, self.cells, self.nx, self.ny = shape
        self.size = self.cells // CHUNKS
        self.block = math.gcd(self.size, 2)
        self.steps = self.size // self.block

    def rows(self, chunk=None):
        base = 0 if chunk is None else chunk * self.steps
        return pl.BlockSpec(
            (self.count, self.block, self.nx, self.ny), lambda i: (0, base + i, 0, 0)
        )

    def whole(self, array):
        return pl.BlockSpec(array.shape, lambda i: (0,) * array.ndim)

    def spectra(self, chunk):
        base = chunk * self.steps
        return pl.BlockSpec((self.block, KX, self.count * KY), lambda i: (base + i, 0, 0))

    def piece(self):
        return jax.ShapeDtypeStruct((self.count, self.size, self.nx, self.ny), jnp.bfloat16)

    def cost(self, arrays, dots):
        cells = self.count * self.size * self.nx * self.ny
        return pl.CostEstimate(
            flops=dots * cells * 2 * self.count * TILE, bytes_accessed=arrays * 2 * cells,
            transcendentals=0,
        )

    def params(self):
        return pltpu.CompilerParams(
            dimension_semantics=("arbitrary",), vmem_limit_bytes=VMEM_BYTES
        )

    def scratch(self):
        return [pltpu.VMEM((self.nx, self.count * self.ny), jnp.float32)]

    def partial(self, weights, own, other, chunk):
        return pl.pallas_call(
            partial_kernel,
            grid=(self.steps,),
            in_specs=[self.whole(weights), self.rows(chunk), self.rows()],
            out_specs=self.rows(),
            out_shape=self.piece(),
            compiler_params=self.params(),
            cost_estimate=self.cost(3, 2),
        )(weights, own, other)

    def forward(self, weights, tables, bias, own, other, part, spec, cot, chunk, held):
        args = [weights, *tables, bias, own, other, part, spec, cot]
        specs = [self.whole(weights), *[self.whole(t) for t in tables]]
        specs += [pl.BlockSpec(memory_space=pltpu.SMEM)]
        specs += [self.rows(chunk), self.rows(), self.rows(), self.spectra(chunk), self.rows(chunk)]
        aliases = {}
        if held is not None:
            aliases = {len(args): 0}
            args.append(held)
            specs.append(pl.BlockSpec(memory_space=pl.ANY))
        return pl.pallas_call(
            forward_kernel,
            grid=(self.steps,),
            in_specs=specs,
            out_specs=[self.rows(chunk), self.rows()],
            out_shape=[jax.ShapeDtypeStruct(self.shape, jnp.bfloat16), self.piece()],
            scratch_shapes=self.scratch(),
            input_output_aliases=aliases,
            compiler_params=self.params(),
            cost_estimate=self.cost(7, 4),
        )(*args)

    def backward(self, weights, tables, own, other, part, spec, chunk, held):
        args = [weights, *tables, own, other, part, spec]
        specs = [self.whole(weights), *[self.whole(t) for t in tables]]
        specs += [self.rows(), self.rows(), self.rows(), self.spectra(chunk)]
        aliases = {}
        if held is not None:
            aliases = {len(args): 0}
            args.append(held)
            specs.append(pl.BlockSpec(memory_space=pl.ANY))
        return pl.pallas_call(
            backward_kernel,
            grid=(self.steps,),
            in_specs=specs,
            out_specs=self.rows(chunk),
            out_shape=jax.ShapeDtypeStruct(self.shape, jnp.bfloat16),
            scratch_shapes=self.scratch(),
            input_output_aliases=aliases,
            compiler_params=self.params(),
            cost_estimate=self.cost(4, 3),
        )(*args)


def spread(matrix):
    eye = jnp.eye(TILE, dtype=matrix.dtype)
    rows, columns = matrix.shape
    return (matrix[:, None, :, None] * eye[None, :, None, :]).reshape(rows * TILE, columns * TILE)


def body(field, spec_weight, mix_weight, bias, cotangent):
    table_x, table_y, table_zt = make_tables()
    full_shape = field.shape
    count = full_shape[0]
    shape = (count, full_shape[1] * full_shape[2], full_shape[3], full_shape[4])
    field = field.reshape(shape)
    cotangent = cotangent.reshape(shape)
    local = Local(shape)
    parts = mix_weight.shape[0] // count
    across = [(i, i ^ 2) for i in range(parts)]
    beside = [(i, i ^ 1) for i in range(parts)]
    me = lax.axis_index("chan")

    eye = jnp.eye(count, dtype=table_y.dtype)
    wide_y = (eye[:, None, :, None] * table_y[None, :, None, :]).reshape(
        count * KY, count * shape[3]
    )
    tables = (table_x.T, wide_y)

    def weights_for(matrix):
        def block(row, column):
            return lax.dynamic_slice(matrix, (row * count, column * count), (count, count))

        return [
            spread(jnp.concatenate([block(row, me), block(row, me ^ 2)], axis=1))
            for row in (me, me ^ 1)
        ]

    own_weights, beside_weights = weights_for(mix_weight)
    own_back, beside_back = weights_for(mix_weight.T)

    def cut(values, chunk):
        return values[:, chunk * local.size : (chunk + 1) * local.size]

    others = [lax.ppermute(cut(field, k), "chan", across) for k in range(CHUNKS)]
    coeffs = analyse_zt(analyse_xy(field, table_x, table_y), table_zt)
    partial_value = jnp.einsum(
        "cokm,ckm->okm", spec_weight, coeffs, preferred_element_type=jnp.float32
    )
    mixed = lax.psum_scatter(
        partial_value.astype(jnp.bfloat16), "chan", scatter_dimension=0, tiled=True
    )
    spectra = synthesise_zt(mixed, table_zt)
    shares = [
        lax.ppermute(local.partial(beside_weights, field, others[k], k), "chan", beside)
        for k in range(CHUNKS)
    ]
    output, grads, seconds, grad_others = None, [], [], []
    for k in range(CHUNKS):
        output, grad = local.forward(
            own_weights, tables, bias, field, others[k], shares[k], spectra, cotangent, k, output
        )
        grads.append(grad)
        grad_others.append(lax.ppermute(grad, "chan", across))
        seconds.append(analyse_xy(grad, table_x, table_y))
    grad_coeffs = analyse_zt(jnp.concatenate(seconds, axis=1), table_zt)
    all_grad = lax.all_gather(grad_coeffs, "chan", axis=0, tiled=True)
    grad_weight = (coeffs.astype(jnp.float32)[:, None] * all_grad.astype(jnp.float32)[None]).astype(
        jnp.bfloat16
    )
    back_coeffs = jnp.einsum(
        "cokm,okm->ckm", spec_weight, all_grad, preferred_element_type=jnp.float32
    ).astype(jnp.bfloat16)
    back = synthesise_zt(back_coeffs, table_zt)
    grad_shares = [
        lax.ppermute(
            local_partial(local, beside_back, grads[k], grad_others[k]), "chan", beside
        )
        for k in range(CHUNKS)
    ]
    grad_field = None
    for k in range(CHUNKS):
        grad_field = local.backward(
            own_back, tables, grads[k], grad_others[k], grad_shares[k], back, k, grad_field
        )
    return (output.reshape(full_shape), grad_field.reshape(full_shape), grad_weight)


def local_partial(local, weights, own, other):
    return local.partial(weights, own, other, 0)


def solution(mesh):
    return jax.shard_map(
        body,
        mesh=mesh,
        in_specs=(
            P(("groups", "chan"), "slab", None, None, None),
            P("chan", None, "slab", None),
            P(),
            P("chan"),
            P(("groups", "chan"), "slab", None, None, None),
        ),
        out_specs=(
            P(("groups", "chan"), "slab", None, None, None),
            P(("groups", "chan"), "slab", None, None, None),
            P(("groups", "chan"), None, "slab", None),
        ),
        check_vma=False,
    )
```

```python
import math

import jax
import jax.numpy as jnp
from jax import lax
from jax.experimental import pallas as pl
from jax.experimental.pallas import tpu as pltpu
from jax.sharding import PartitionSpec as P

NX = 128
NY = 128
NZ = 64
NT = 4
KX = 32
KY = 32
KZ = 32
TILE = 16
VMEM_BYTES = 40 * 1024 * 1024


def fourier_rows(count, length):
    rows = jnp.arange(count)
    points = jnp.arange(length)
    freq = (rows + 1) // 2
    phase = freq[:, None] * points[None, :] % length
    angle = phase.astype(jnp.float32) * (2.0 * math.pi / length)
    use_cos = (rows % 2 == 1) | (rows == 0)
    table = jnp.where(use_cos[:, None], jnp.cos(angle), jnp.sin(angle))
    return table * math.sqrt(2.0 / length)


def make_tables():
    table_x = fourier_rows(KX, NX).astype(jnp.bfloat16)
    table_y = fourier_rows(KY, NY).astype(jnp.bfloat16)
    depth = fourier_rows(KZ, NZ)
    times = fourier_rows(NT, NT)
    table_zt = (depth[:, None, :, None] * times[None, :, None, :]).reshape(KZ * NT, NZ * NT)
    return (table_x, table_y, table_zt.astype(jnp.bfloat16))


def analyse_zt(second, table_zt, count):
    if KX % lax.axis_size("slab"):
        second = second.reshape(second.shape[0], KX, count, KY).transpose(2, 0, 1, 3)
        second = second.reshape(count, second.shape[1], KX * KY)
        owned = lax.all_to_all(second, "slab", split_axis=2, concat_axis=1, tiled=True)
        coeffs = jnp.einsum("mz,czk->ckm", table_zt, owned, preferred_element_type=jnp.float32)
        return coeffs.astype(jnp.bfloat16)
    owned = lax.all_to_all(second, "slab", split_axis=1, concat_axis=0, tiled=True)
    cells, own_x, _ = owned.shape
    owned = owned.reshape(cells, own_x, count, KY)
    coeffs = jnp.einsum("mz,zjck->cjkm", table_zt, owned, preferred_element_type=jnp.float32)
    return coeffs.astype(jnp.bfloat16).reshape(count, own_x * KY, table_zt.shape[0])


def synthesise_zt(coeffs, table_zt):
    count, modes, _ = coeffs.shape
    if KX % lax.axis_size("slab"):
        slabs = jnp.einsum("mz,okm->ozk", table_zt, coeffs, preferred_element_type=jnp.float32)
        slabs = slabs.astype(jnp.bfloat16)
        local = lax.all_to_all(slabs, "slab", split_axis=1, concat_axis=2, tiled=True)
        local = local.reshape(count, local.shape[1], KX, KY).transpose(1, 2, 0, 3)
        return local.reshape(local.shape[0], KX, count * KY)
    coeffs = coeffs.reshape(count, modes // KY, KY, coeffs.shape[2])
    slabs = jnp.einsum("mz,ojkm->zjok", table_zt, coeffs, preferred_element_type=jnp.float32)
    slabs = slabs.astype(jnp.bfloat16).reshape(slabs.shape[0], modes // KY, count * KY)
    return lax.all_to_all(slabs, "slab", split_axis=0, concat_axis=1, tiled=True)


def mix_pair(own_ref, other_ref, weights, row, pair):
    halves = []
    for half in range(2):
        lines = pl.ds((2 * pair + half) * TILE, TILE)
        mine = own_ref[:, row, lines, :]
        theirs = other_ref[:, row, lines, :]
        shape = (mine.shape[0] * TILE, mine.shape[2])
        halves.append(jnp.concatenate([mine.reshape(shape), theirs.reshape(shape)], axis=0))
    return jnp.dot(
        weights, jnp.concatenate(halves, axis=1), preferred_element_type=jnp.float32
    )


def spectral_rows(spec_ref, tx_ref, ty_ref, row):
    first = jnp.dot(tx_ref[...], spec_ref[row], preferred_element_type=jnp.float32)
    return jnp.dot(
        first.astype(jnp.bfloat16), ty_ref[...], preferred_element_type=jnp.float32
    )


def analyse_row(values_ref, ax_ref, ay_ref, row):
    count = values_ref.shape[0]
    values = jnp.concatenate([values_ref[c, row] for c in range(count)], axis=1)
    first = jnp.dot(ax_ref[...], values, preferred_element_type=jnp.float32)
    return jnp.dot(
        first.astype(jnp.bfloat16), ay_ref[...], preferred_element_type=jnp.float32
    ).astype(jnp.bfloat16)


def analysis_kernel(ax_ref, ay_ref, field_ref, second_ref):
    for row in range(field_ref.shape[1]):
        second_ref[row] = analyse_row(field_ref, ax_ref, ay_ref, row)


def gate_kernel(value_ref, *refs):
    refs[-1][...] = value_ref[...]


def gate(value, *earlier):
    return pl.pallas_call(
        gate_kernel,
        in_specs=[pl.BlockSpec(memory_space=pltpu.VMEM)]
        + [pl.BlockSpec(memory_space=pl.ANY) for _ in earlier],
        out_specs=pl.BlockSpec(memory_space=pltpu.VMEM),
        out_shape=jax.ShapeDtypeStruct(value.shape, value.dtype),
        compiler_params=pltpu.CompilerParams(vmem_limit_bytes=VMEM_BYTES),
    )(value, *earlier)


def partial_kernel(weight_ref, own_ref, other_ref, token_ref, spec_ref, out_ref, done_ref):
    done_ref[...] = jnp.zeros_like(done_ref)
    weights = weight_ref[...]
    count, rows, nx, ny = out_ref.shape
    for row in range(rows):
        for pair in range(nx // (2 * TILE)):
            mixed = mix_pair(own_ref, other_ref, weights, row, pair).astype(jnp.bfloat16)
            for half in range(2):
                part = mixed[:, half * ny : (half + 1) * ny]
                out_ref[:, row, pl.ds((2 * pair + half) * TILE, TILE), :] = part.reshape(
                    count, TILE, ny
                )


def forward_kernel(*refs):
    weight_ref, tx_ref, ty_ref, ax_ref, ay_ref, bias_ref = refs[:6]
    own_ref, other_ref, part_ref, spec_ref, cot_ref = refs[6:11]
    out_ref, grad_ref, second_ref, done_ref, pre_ref = refs[-5:]
    done_ref[...] = jnp.zeros_like(done_ref)
    weights = weight_ref[...]
    count, rows, nx, ny = out_ref.shape
    scale = math.sqrt(2.0 / math.pi)
    cubic = 0.044715
    for row in range(rows):
        pre_ref[...] = spectral_rows(spec_ref, tx_ref, ty_ref, row)
        for pair in range(nx // (2 * TILE)):
            mixed = mix_pair(own_ref, other_ref, weights, row, pair)
            for half in range(2):
                lines = pl.ds((2 * pair + half) * TILE, TILE)
                for o in range(count):
                    pre = (
                        mixed[o * TILE : (o + 1) * TILE, half * ny : (half + 1) * ny]
                        + pre_ref[lines, o * ny : (o + 1) * ny]
                        + part_ref[o, row, lines, :].astype(jnp.float32)
                        + bias_ref[o]
                    )
                    square = pre * pre
                    bent = jnp.tanh(scale * (pre + cubic * (pre * square)))
                    half_up = 0.5 * (1.0 + bent)
                    slope = half_up + (0.5 * pre) * (1.0 - bent * bent) * (
                        scale * (1.0 + (3.0 * cubic) * square)
                    )
                    out_ref[o, row, lines, :] = (pre * half_up).astype(jnp.bfloat16)
                    cot = cot_ref[o, row, lines, :].astype(jnp.float32)
                    grad_ref[o, row, lines, :] = (cot * slope).astype(jnp.bfloat16)
        second_ref[row] = analyse_row(grad_ref, ax_ref, ay_ref, row)


def backward_kernel(*refs):
    weight_ref, tx_ref, ty_ref, own_ref, other_ref, part_ref, spec_ref = refs[:7]
    out_ref, done_ref, pre_ref = refs[-3:]
    done_ref[...] = jnp.zeros_like(done_ref)
    weights = weight_ref[...]
    count, rows, nx, ny = out_ref.shape
    for row in range(rows):
        pre_ref[...] = spectral_rows(spec_ref, tx_ref, ty_ref, row)
        for pair in range(nx // (2 * TILE)):
            mixed = mix_pair(own_ref, other_ref, weights, row, pair)
            for half in range(2):
                lines = pl.ds((2 * pair + half) * TILE, TILE)
                for o in range(count):
                    total = (
                        mixed[o * TILE : (o + 1) * TILE, half * ny : (half + 1) * ny]
                        + pre_ref[lines, o * ny : (o + 1) * ny]
                        + part_ref[o, row, lines, :].astype(jnp.float32)
                    )
                    out_ref[o, row, lines, :] = total.astype(jnp.bfloat16)


class Local:
    def __init__(self, shape, start, size):
        self.shape = shape
        self.count, self.cells, self.nx, self.ny = shape
        self.start, self.size = start, size
        self.block = math.gcd(math.gcd(start, size), 4)
        self.steps = size // self.block

    def rows(self, inside=False):
        base = self.start // self.block if inside else 0
        return pl.BlockSpec(
            (self.count, self.block, self.nx, self.ny), lambda i: (0, base + i, 0, 0)
        )

    def whole(self, array):
        return pl.BlockSpec(array.shape, lambda i: (0,) * array.ndim)

    def spectra(self, inside=False):
        base = self.start // self.block if inside else 0
        return pl.BlockSpec((self.block, KX, self.count * KY), lambda i: (base + i, 0, 0))

    def piece(self):
        return jax.ShapeDtypeStruct((self.count, self.size, self.nx, self.ny), jnp.bfloat16)

    def cost(self):
        return pl.CostEstimate(flops=1, bytes_accessed=1, transcendentals=0)

    def params(self):
        return pltpu.CompilerParams(
            dimension_semantics=("arbitrary",), vmem_limit_bytes=VMEM_BYTES
        )

    def scratch(self):
        return [pltpu.VMEM((self.nx, self.count * self.ny), jnp.float32)]

    def token(self):
        return jax.ShapeDtypeStruct((8, 128), jnp.float32)

    def token_spec(self):
        return pl.BlockSpec((8, 128), lambda i: (0, 0))

    def second(self):
        return jax.ShapeDtypeStruct((self.size, KX, self.count * KY), jnp.bfloat16)

    def analysis(self, tables, field):
        return pl.pallas_call(
            analysis_kernel,
            grid=(self.steps,),
            in_specs=[*[self.whole(t) for t in tables], self.rows()],
            out_specs=self.spectra(),
            out_shape=self.second(),
            compiler_params=self.params(),
            cost_estimate=self.cost(),
        )(*tables, field)

    def partial(self, weights, own, other, inside, token, spec):
        return pl.pallas_call(
            partial_kernel,
            grid=(self.steps,),
            in_specs=[
                self.whole(weights),
                self.rows(inside),
                self.rows(inside),
                self.token_spec(),
                pl.BlockSpec(memory_space=pl.ANY),
            ],
            out_specs=[self.rows(), self.token_spec()],
            out_shape=[self.piece(), self.token()],
            compiler_params=self.params(),
            cost_estimate=self.cost(),
        )(weights, own, other, token, spec)

    def forward(
        self, weights, tables, bias, own, other, part, spec, cot, token, held, earlier
    ):
        args = [weights, *tables, bias, own, other, part, spec, cot, token, earlier]
        specs = [self.whole(weights), *[self.whole(t) for t in tables]]
        specs += [pl.BlockSpec(memory_space=pltpu.SMEM)]
        specs += [self.rows(True), self.rows(True), self.rows(), self.spectra(True), self.rows(True)]
        specs += [self.token_spec(), pl.BlockSpec(memory_space=pl.ANY)]
        aliases = {}
        if held is not None:
            aliases = {len(args): 0}
            args.append(held)
            specs.append(pl.BlockSpec(memory_space=pl.ANY))
        return pl.pallas_call(
            forward_kernel,
            grid=(self.steps,),
            in_specs=specs,
            out_specs=[self.rows(True), self.rows(), self.spectra(), self.token_spec()],
            out_shape=[
                jax.ShapeDtypeStruct(self.shape, jnp.bfloat16),
                self.piece(),
                self.second(),
                self.token(),
            ],
            scratch_shapes=self.scratch(),
            input_output_aliases=aliases,
            compiler_params=self.params(),
            cost_estimate=self.cost(),
        )(*args)

    def backward(self, weights, tables, own, other, part, spec, token, held):
        args = [weights, *tables, own, other, part, spec, token]
        specs = [self.whole(weights), *[self.whole(t) for t in tables]]
        specs += [self.rows(), self.rows(), self.rows(), self.spectra(True), self.token_spec()]
        aliases = {}
        if held is not None:
            aliases = {len(args): 0}
            args.append(held)
            specs.append(pl.BlockSpec(memory_space=pl.ANY))
        return pl.pallas_call(
            backward_kernel,
            grid=(self.steps,),
            in_specs=specs,
            out_specs=[self.rows(True), self.token_spec()],
            out_shape=[jax.ShapeDtypeStruct(self.shape, jnp.bfloat16), self.token()],
            scratch_shapes=self.scratch(),
            input_output_aliases=aliases,
            compiler_params=self.params(),
            cost_estimate=self.cost(),
        )(*args)


def spread(matrix):
    eye = jnp.eye(TILE, dtype=matrix.dtype)
    rows, columns = matrix.shape
    return (matrix[:, None, :, None] * eye[None, :, None, :]).reshape(rows * TILE, columns * TILE)


def body(field, spec_weight, mix_weight, bias, cotangent):
    table_x, table_y, table_zt = make_tables()
    full_shape = field.shape
    count = full_shape[0]
    shape = (count, full_shape[1] * full_shape[2], full_shape[3], full_shape[4])
    field = field.reshape(shape)
    cotangent = cotangent.reshape(shape)
    unit = max(shape[1] // 8, 1)
    ends = [0, 2 * unit, max(shape[1] - unit, 2 * unit), shape[1]]
    spans = [Local(shape, a, b - a) for a, b in zip(ends, ends[1:]) if b > a]
    chunks = len(spans)
    parts = mix_weight.shape[0] // count
    across = [(i, i ^ 2) for i in range(parts)]
    beside = [(i, i ^ 1) for i in range(parts)]
    me = lax.axis_index("chan")

    eye = jnp.eye(count, dtype=table_y.dtype)
    wide_y = (eye[:, None, :, None] * table_y[None, :, None, :]).reshape(
        count * KY, count * shape[3]
    )
    synthesis_tables = (table_x.T, wide_y)
    analysis_tables = (table_x, wide_y.T)

    def weights_for(matrix):
        def block(row, column):
            return lax.dynamic_slice(matrix, (row * count, column * count), (count, count))

        return [
            spread(jnp.concatenate([block(row, me), block(row, me ^ 2)], axis=1))
            for row in (me, me ^ 1)
        ]

    own_weights, beside_weights = weights_for(mix_weight)
    own_back, beside_back = weights_for(mix_weight.T)

    token = jnp.zeros((8, 128), jnp.float32)
    other = lax.ppermute(field, "chan", across)
    second = Local(shape, 0, shape[1]).analysis(analysis_tables, field)
    coeffs = analyse_zt(second, table_zt, count)
    partial_value = jnp.einsum(
        "cokm,ckm->okm", spec_weight, coeffs, preferred_element_type=jnp.float32
    )
    mixed = lax.psum_scatter(
        partial_value.astype(jnp.bfloat16), "chan", scatter_dimension=0, tiled=True
    )
    spectra = synthesise_zt(mixed, table_zt)

    def share(k, token):
        part, token = spans[k].partial(beside_weights, field, other, True, token, spectra)
        return lax.ppermute(part, "chan", beside), token

    output, grads, seconds, grad_others = None, [], [], []
    tables = (*synthesis_tables, *analysis_tables)
    now, token = share(0, token)
    for k in range(chunks):
        later = None
        if k + 1 < chunks:
            later, token = share(k + 1, token)
        output, grad, second, token = spans[k].forward(
            own_weights, tables, bias, field, other, now, spectra, cotangent, token, output,
            token,
        )
        now = later
        grads.append(grad)
        grad_others.append(lax.ppermute(grad, "chan", across))
        seconds.append(second)
    second = jnp.concatenate(seconds, axis=0)
    grad_coeffs = analyse_zt(second, table_zt, count)
    all_grad = gate(lax.all_gather(grad_coeffs, "chan", axis=0, tiled=True), grad_others[min(1, chunks - 1)])
    grad_weight = (coeffs.astype(jnp.float32)[:, None] * all_grad.astype(jnp.float32)[None]).astype(
        jnp.bfloat16
    )
    back_coeffs = jnp.einsum(
        "cokm,okm->ckm", spec_weight, all_grad, preferred_element_type=jnp.float32
    ).astype(jnp.bfloat16)
    back = synthesise_zt(back_coeffs, table_zt)

    def share_back(k, token):
        part, token = spans[k].partial(beside_back, grads[k], grad_others[k], False, token, back)
        return lax.ppermute(part, "chan", beside), token

    grad_field = None
    now, token = share_back(0, token)
    for k in range(chunks):
        later = None
        if k + 1 < chunks:
            later, token = share_back(k + 1, token)
        grad_field, token = spans[k].backward(
            own_back, synthesis_tables, grads[k], grad_others[k], now, back, token, grad_field
        )
        now = later
    return (output.reshape(full_shape), grad_field.reshape(full_shape), grad_weight)


def solution(mesh):
    return jax.shard_map(
        body,
        mesh=mesh,
        in_specs=(
            P(("groups", "chan"), "slab", None, None, None),
            P("chan", None, "slab", None),
            P(),
            P("chan"),
            P(("groups", "chan"), "slab", None, None, None),
        ),
        out_specs=(
            P(("groups", "chan"), "slab", None, None, None),
            P(("groups", "chan"), "slab", None, None, None),
            P(("groups", "chan"), None, "slab", None),
        ),
        check_vma=False,
    )
```
